256 devices in a mesh: loop: 64 (over x_lo, z, y), team: 4 (over x_hi, core).
Axes of the slice: x: 4 (x_hi: 2, x_lo: 2; x = x_hi * 2 + x_lo), y: 4, z: 8, core: 2. Of those that a mesh axis runs over, the one named last changes fastest.
Arguments:
- samples: bfloat16 [4096, 11776], P(('loop', 'team')), may hold values from -6 to 6
- input_gains: float32 [2, 4096, 4, 128], P(None, 'loop', None, 'team'), may hold values from -5 to 5
Outputs:
- visibility: float32 [64, 4, 2, 256, 4096], P('loop', 'team')
The draws below stay inside these ranges and needn't reach their ends.
All inputs are finite; a program needn't handle non-finite values.
Results may differ from the reference program's by a relative error of at most 0.0038.
Values may be sent and summed in bfloat16 or wider, within the bound.
No kernel may reach another device: no remote copies, remote signals or barrier semaphores. Data moves between devices by JAX's collectives and lax.ppermute only.
A program may use at most 64 MiB of HBM per device.

```python
import math
import jax
import jax.numpy as jnp
from jax import lax

FCH = 512
TAPS = 8
AVG = 32
SPEC = 16
ROWS_DEV = 256
BINS = 16
BSUB = 4
GROUPS = 16
NIN = 4096
NSAMP = 11776
N_LOOP = 64
N_TEAM = 4


def steps_of(key, shape, pieces, least, high):
    factor_of = 1.0
    for dim, blocks in pieces:
        heights = jax.random.uniform(jax.random.fold_in(jax.random.fold_in(key, 6), dim), (blocks,), jnp.float32, least / len(pieces), high / len(pieces))
        factor_of = factor_of * jnp.repeat(jnp.exp(heights), shape[dim] // blocks).reshape((-1,) + (1,) * (len(shape) - 1 - dim))
    return factor_of


def gaussian(stream_key, extent, scale, limit, split=(), kind=jnp.bfloat16):
    result = jax.random.normal(stream_key, extent, jnp.float32) * scale
    if len(split) > 0:
        result = steps_of(stream_key, extent, split, -0.22, 0.18) * result
    return jnp.clip(result, min=-limit, max=limit).astype(kind)


def setup_inputs(seed: int = 0) -> dict:
    streams_of = jax.random.split(jax.random.key(seed), 3)
    samples = gaussian(streams_of[0], (NIN, NSAMP), 1.0, 6.0, ((0, 256),))
    input_gains = gaussian(streams_of[1], (2, NIN, BSUB, FCH // BSUB), 1.0, 5.0, ((1, 64), (3, 4)), jnp.float32)
    return {"samples": samples, "input_gains": input_gains}


def pfb_window():
    sample_pos = jnp.arange(TAPS * FCH, dtype=jnp.float32) + 0.5
    taper = jnp.sin(jnp.pi * sample_pos / (TAPS * FCH)) ** 2
    taps_table = jnp.sinc(sample_pos / FCH - TAPS / 2) * taper
    return taps_table.reshape(TAPS, FCH)

def reference(samples, input_gains):
    frames = samples.astype(jnp.float32).reshape(NIN, SPEC + TAPS - 1, FCH)
    window = pfb_window()
    filtered = jnp.zeros((NIN, SPEC, FCH), jnp.float32)
    for tap_index in range(TAPS):
        filtered = filtered + window[tap_index] * frames[:, tap_index:tap_index + SPEC, :]
    spectrum = jnp.fft.fft(filtered, axis=-1) / math.sqrt(FCH)
    real_part = jnp.real(spectrum)
    imag_part = jnp.imag(spectrum)
    gains_flat = input_gains.reshape(2, NIN, FCH)
    gain_re = gains_flat[0][:, None, :]
    gain_im = gains_flat[1][:, None, :]
    volt_re = (gain_re * real_part - gain_im * imag_part).astype(jnp.bfloat16)
    volt_im = (gain_re * imag_part + gain_im * real_part).astype(jnp.bfloat16)
    stacked = jnp.stack([volt_re, volt_im], axis=1)
    packed = stacked.reshape(NIN, 2, SPEC, BINS, AVG).transpose(3, 0, 1, 2, 4).reshape(BINS, NIN, 2 * SPEC * AVG)
    half_width = SPEC * AVG
    norm_scale = 1.0 / (AVG * SPEC)
    columns = packed.astype(jnp.float32)

    def one_group(group_index):
        rows_part = lax.dynamic_slice_in_dim(columns, (group_index * ROWS_DEV).astype(jnp.int32), ROWS_DEV, 1)
        rotated = jnp.concatenate([rows_part[..., half_width:], -rows_part[..., :half_width]], axis=-1)
        real_vis = jnp.einsum('brk,bjk->brj', rows_part, columns, precision=lax.Precision.HIGHEST, preferred_element_type=jnp.float32)
        imag_vis = jnp.einsum('brk,bjk->brj', rotated, columns, precision=lax.Precision.HIGHEST, preferred_element_type=jnp.float32)
        return jnp.stack([real_vis, imag_vis], axis=1) * norm_scale
    every_group = lax.map(one_group, jnp.arange(GROUPS, dtype=jnp.int32))
    return every_group.reshape(N_LOOP, N_TEAM, 2, ROWS_DEV, NIN)
```

```python
import math

import jax
import jax.numpy as jnp
import numpy as np
from jax import lax
from jax.sharding import Mesh
from jax.sharding import PartitionSpec as P

FCH = 512
TAPS = 8
AVG = 32
SPEC = 16
SCALE = 1.0 / (AVG * SPEC)


def ring_pairs(count, by):
    return [(i, (i + by) % count) for i in range(count)]


def xor_pairs(count, by):
    return [(i, i ^ by) for i in range(count)]


def pfb_window():
    sample_pos = jnp.arange(TAPS * FCH, dtype=jnp.float32) + 0.5
    taper = jnp.sin(jnp.pi * sample_pos / (TAPS * FCH)) ** 2
    taps_table = jnp.sinc(sample_pos / FCH - TAPS / 2) * taper
    return taps_table.reshape(TAPS, FCH)


def dft_table():
    position = np.arange(FCH)
    angle = (position[:, None] * position[None, :] % FCH) * (2.0 * math.pi / FCH)
    table = np.concatenate([np.cos(angle), -np.sin(angle)], axis=1) / math.sqrt(FCH)
    return jnp.asarray(table.astype(np.float32))


def pick(stacked, slot):
    return lax.dynamic_index_in_dim(stacked, slot, 0, keepdims=False)


def exchange(pieces, axis, place):
    count = pieces.shape[0]
    received = [pick(pieces, place)]
    for by in range(1, count):
        received.append(lax.ppermute(pick(pieces, place ^ by), axis, xor_pairs(count, by)))
    stacked = jnp.stack(received)
    return jnp.stack([pick(stacked, place ^ i) for i in range(count)])


def spectra(samples):
    rows = samples.shape[0]
    frames = samples.astype(jnp.float32).reshape(rows, SPEC + TAPS - 1, FCH)
    window = pfb_window()
    filtered = window[0] * frames[:, 0:SPEC, :]
    for tap in range(1, TAPS):
        filtered = filtered + window[tap] * frames[:, tap : tap + SPEC, :]
    return jnp.einsum(
        "itp,pc->itc",
        filtered,
        dft_table(),
        precision=lax.Precision.HIGH,
        preferred_element_type=jnp.float32,
    )


def turned(block):
    half = block.shape[1] // 2
    return jnp.concatenate([block[:, half:], -block[:, :half]], axis=1)


def local(samples, input_gains):
    team = ("xh", "c")
    member = lax.axis_index(team)
    y_place = lax.axis_index("y")
    z_place = lax.axis_index("z")
    x_place = lax.axis_index("xl")
    members = lax.axis_size(team)
    bins = input_gains.shape[2]
    z_size = lax.axis_size("z")
    rows = samples.shape[0]

    gain_parts = input_gains.reshape(2, members, rows, bins * AVG).transpose(1, 0, 2, 3)
    gains = exchange(gain_parts, team, member)
    gains = gains.reshape(members, 2, rows, bins, AVG).transpose(1, 2, 3, 0, 4)

    shaped = spectra(samples).reshape(rows, SPEC, 2, bins, members, AVG)
    real, imag = shaped[:, :, 0], shaped[:, :, 1]
    gain_re, gain_im = gains[0][:, None], gains[1][:, None]
    volt_re = (gain_re * real - gain_im * imag).astype(jnp.bfloat16)
    volt_im = (gain_re * imag + gain_im * real).astype(jnp.bfloat16)
    packed = jnp.stack([volt_re, volt_im], axis=1)
    packed = packed.transpose(4, 3, 0, 1, 2, 5)
    packed = packed.reshape(members, bins, rows, 2 * SPEC * AVG)

    by_member = exchange(packed, team, member)
    by_bin = by_member.transpose(1, 0, 2, 3).reshape(bins, members * rows, -1)
    block = exchange(by_bin, "y", y_place)
    block = block.reshape(bins * members * rows, -1)
    height = block.shape[0]

    other = lax.ppermute(block, "xl", ring_pairs(2, 1))
    own_left = jnp.concatenate([block, turned(block)], axis=0)
    other_left = jnp.concatenate([other, turned(other)], axis=0)

    visibility = jnp.zeros((2, height, height * z_size * 2), jnp.float32)

    def product(lhs, columns):
        return (
            jnp.einsum("rk,pk->rp", lhs, columns, preferred_element_type=jnp.float32) * SCALE
        )

    def place(state, values, group):
        values = values.astype(jnp.float32).reshape(2, height, -1)
        nought = jnp.zeros((), jnp.int32)
        return lax.dynamic_update_slice(state, values, (nought, nought, group * height))

    visibility = place(visibility, product(own_left, block), x_place * z_size + z_place)
    visibility = place(visibility, product(own_left, other), (1 - x_place) * z_size + z_place)

    ahead, behind = block, block
    for step in range(1, z_size // 2 + 1):
        if step < z_size // 2:
            ahead = lax.ppermute(ahead, "z", ring_pairs(z_size, 1))
            behind = lax.ppermute(behind, "z", ring_pairs(z_size, -1))
            arrived = [(ahead, (z_place - step) % z_size), (behind, (z_place + step) % z_size)]
        else:
            half = height // 2
            upper = lax.ppermute(ahead[:half], "z", ring_pairs(z_size, 1))
            lower = lax.ppermute(behind[half:], "z", ring_pairs(z_size, -1))
            arrived = [(jnp.concatenate([upper, lower], axis=0), (z_place + step) % z_size)]
        made = [product(other_left, columns).astype(jnp.bfloat16) for columns, _ in arrived]
        given = lax.ppermute(jnp.stack(made), "xl", ring_pairs(2, 1))
        for index, (columns, group) in enumerate(arrived):
            visibility = place(visibility, product(own_left, columns), x_place * z_size + group)
            visibility = place(visibility, given[index], (1 - x_place) * z_size + group)
    return visibility[None, None]


def solution(mesh):
    fine = Mesh(
        mesh.devices.reshape(2, 8, 4, 2, 2), ("xl", "z", "y", "xh", "c")
    )
    everything = ("xl", "z", "y", "xh", "c")
    return jax.shard_map(
        local,
        mesh=fine,
        in_specs=(P(everything, None), P(None, ("xl", "z", "y"), None, ("xh", "c"))),
        out_specs=P(("xl", "z", "y"), ("xh", "c"), None, None, None),
        check_vma=False,
    )
```

```python
import math

import jax
import jax.numpy as jnp
import ml_dtypes
import numpy as np
from jax import lax
from jax.experimental import pallas as pl
from jax.experimental.pallas import tpu as pltpu
from jax.sharding import Mesh
from jax.sharding import PartitionSpec as P

FCH = 512
TAPS = 8
AVG = 32
SPEC = 16
SCALE = 1.0 / (AVG * SPEC)


def ring_pairs(count, by):
    return [(i, (i + by) % count) for i in range(count)]


def xor_pairs(count, by):
    return [(i, i ^ by) for i in range(count)]


def pfb_window():
    position = np.arange(TAPS * FCH) + 0.5
    taper = np.sin(np.pi * position / (TAPS * FCH)) ** 2
    table = np.sinc(position / FCH - TAPS / 2) * taper
    return table.reshape(TAPS, FCH).astype(np.float32)


def dft_table():
    position = np.arange(FCH)
    angle = (position[:, None] * position[None, :] % FCH) * (2.0 * math.pi / FCH)
    table = np.concatenate([np.cos(angle), -np.sin(angle)], axis=1) / math.sqrt(FCH)
    upper = table.astype(ml_dtypes.bfloat16)
    lower = (table - upper.astype(np.float64)).astype(ml_dtypes.bfloat16)
    return np.concatenate([upper, lower, upper], axis=0)


def pick(stacked, slot):
    return lax.dynamic_index_in_dim(stacked, slot, 0, keepdims=False)


def exchange(pieces, axis):
    count = len(pieces)
    return [pieces[0]] + [
        lax.ppermute(pieces[by], axis, xor_pairs(count, by)) for by in range(1, count)
    ]


def in_order(received, place):
    stacked = jnp.stack(received)
    return jnp.stack([pick(stacked, place ^ i) for i in range(len(received))])


def spectra_kernel(samples_ref, window_ref, table_ref, out_ref, filtered):
    rows = samples_ref.shape[0]
    frames = [
        samples_ref[:, f * FCH : (f + 1) * FCH].astype(jnp.float32)
        for f in range(SPEC + TAPS - 1)
    ]
    for t in range(SPEC):
        total = window_ref[0:1, :] * frames[t]
        for tap in range(1, TAPS):
            total = total + window_ref[tap : tap + 1, :] * frames[t + tap]
        upper = total.astype(jnp.bfloat16)
        lower = (total - upper.astype(jnp.float32)).astype(jnp.bfloat16)
        here = slice(t * rows, (t + 1) * rows)
        filtered[here, 0:FCH] = upper
        filtered[here, FCH : 2 * FCH] = upper
        filtered[here, 2 * FCH : 3 * FCH] = lower
    out_ref[...] = jnp.dot(
        filtered[...], table_ref[...], preferred_element_type=jnp.float32
    )


def spectra(samples):
    rows = samples.shape[0]
    return pl.pallas_call(
        spectra_kernel,
        out_shape=jax.ShapeDtypeStruct((SPEC * rows, 2 * FCH), jnp.float32),
        scratch_shapes=[pltpu.VMEM((SPEC * rows, 3 * FCH), jnp.bfloat16)],
        name="spectra",
    )(samples, jnp.asarray(pfb_window()), jnp.asarray(dft_table()))


def quarters(parts, lane):
    joined = parts[3]
    for i in (2, 1, 0):
        joined = jnp.where(lane < (i + 1) * AVG, parts[i], joined)
    return joined


def voltages_kernel(place_ref, spectra_ref, *refs):
    gain_refs, out_refs, (gains, staged) = refs[0:4], refs[4:8], refs[8:]
    rows = gain_refs[0].shape[1]
    member = place_ref[0]
    lanes = 4 * AVG
    lane = lax.broadcasted_iota(jnp.int32, (rows, lanes), 1)
    for by in range(4):
        gains[member ^ by] = gain_refs[by][...]
    for s in range(4):
        gain = [
            quarters(
                [pltpu.roll(gains[m, part], (m - s) * AVG % lanes, 1) for m in range(4)], lane
            )
            for part in range(2)
        ]
        band = slice(s * lanes, (s + 1) * lanes)
        for first in range(0, SPEC, 4):
            turned_re, turned_im = [], []
            for q in range(4):
                here = slice((first + q) * rows, (first + q + 1) * rows)
                real = spectra_ref[here, band]
                imag = spectra_ref[here, FCH + s * lanes : FCH + (s + 1) * lanes]
                volt_re = gain[0] * real - gain[1] * imag
                volt_im = gain[0] * imag + gain[1] * real
                turned_re.append(pltpu.roll(volt_re, q * AVG, 1) if q else volt_re)
                turned_im.append(pltpu.roll(volt_im, q * AVG, 1) if q else volt_im)
            for m in range(4):
                for part, turned_part in enumerate((turned_re, turned_im)):
                    values = quarters([turned_part[(i - m) % 4] for i in range(4)], lane)
                    start = part * SPEC * AVG + first * AVG
                    staged[m, s, :, start : start + lanes] = values.astype(jnp.bfloat16)
    for by in range(4):
        out_refs[by][...] = staged[member ^ by]


def voltages(member, spectra_here, gain_parts):
    rows = gain_parts[0].shape[1]
    piece = jax.ShapeDtypeStruct((4, rows, 2 * SPEC * AVG), jnp.bfloat16)
    vmem = pl.BlockSpec(memory_space=pltpu.VMEM)
    return pl.pallas_call(
        voltages_kernel,
        in_specs=[pl.BlockSpec(memory_space=pltpu.SMEM)] + [vmem] * 5,
        out_specs=[vmem] * 4,
        out_shape=[piece] * 4,
        scratch_shapes=[
            pltpu.VMEM((4,) + gain_parts[0].shape, jnp.float32),
            pltpu.VMEM((4,) + piece.shape, jnp.bfloat16),
        ],
        name="voltages",
    )(member.reshape(1), spectra_here, *gain_parts)


def turned(block):
    half = block.shape[1] // 2
    return jnp.concatenate([block[:, half:], -block[:, :half]], axis=1)


def local(samples, input_gains):
    team = ("xh", "c")
    member = lax.axis_index(team)
    y_place = lax.axis_index("y")
    z_place = lax.axis_index("z")
    x_place = lax.axis_index("xl")
    members = lax.axis_size(team)
    bins = input_gains.shape[2]
    z_size = lax.axis_size("z")
    rows = samples.shape[0]

    gain_parts = input_gains.reshape(2, members, rows, bins * AVG).transpose(1, 0, 2, 3)
    gain_parts = exchange([pick(gain_parts, member ^ by) for by in range(members)], team)
    by_member = in_order(
        exchange(voltages(member, spectra(samples), gain_parts), team), member
    )
    by_bin = by_member.transpose(1, 0, 2, 3).reshape(bins, members * rows, -1)
    block = in_order(exchange([pick(by_bin, y_place ^ by) for by in range(bins)], "y"), y_place)
    block = block.reshape(bins * members * rows, -1)
    height = block.shape[0]

    other = lax.ppermute(block, "xl", ring_pairs(2, 1))
    own_left = jnp.concatenate([block, turned(block)], axis=0)
    other_left = jnp.concatenate([other, turned(other)], axis=0)

    visibility = jnp.zeros((2, height, height * z_size * 2), jnp.float32)

    def product(lhs, columns):
        return (
            jnp.einsum("rk,pk->rp", lhs, columns, preferred_element_type=jnp.float32) * SCALE
        )

    def place(state, values, group):
        values = values.astype(jnp.float32).reshape(2, height, -1)
        nought = jnp.zeros((), jnp.int32)
        return lax.dynamic_update_slice(state, values, (nought, nought, group * height))

    visibility = place(visibility, product(own_left, block), x_place * z_size + z_place)
    visibility = place(visibility, product(own_left, other), (1 - x_place) * z_size + z_place)

    ahead, behind = block, block
    for step in range(1, z_size // 2 + 1):
        if step < z_size // 2:
            ahead = lax.ppermute(ahead, "z", ring_pairs(z_size, 1))
            behind = lax.ppermute(behind, "z", ring_pairs(z_size, -1))
            arrived = [(ahead, (z_place - step) % z_size), (behind, (z_place + step) % z_size)]
        else:
            half = height // 2
            upper = lax.ppermute(ahead[:half], "z", ring_pairs(z_size, 1))
            lower = lax.ppermute(behind[half:], "z", ring_pairs(z_size, -1))
            arrived = [(jnp.concatenate([upper, lower], axis=0), (z_place + step) % z_size)]
        made = [product(other_left, columns).astype(jnp.bfloat16) for columns, _ in arrived]
        given = lax.ppermute(jnp.stack(made), "xl", ring_pairs(2, 1))
        for index, (columns, group) in enumerate(arrived):
            visibility = place(visibility, product(own_left, columns), x_place * z_size + group)
            visibility = place(visibility, given[index], (1 - x_place) * z_size + group)
    return visibility[None, None]


def solution(mesh):
    fine = Mesh(
        mesh.devices.reshape(2, 8, 4, 2, 2), ("xl", "z", "y", "xh", "c")
    )
    everything = ("xl", "z", "y", "xh", "c")
    return jax.shard_map(
        local,
        mesh=fine,
        in_specs=(P(everything, None), P(None, ("xl", "z", "y"), None, ("xh", "c"))),
        out_specs=P(("xl", "z", "y"), ("xh", "c"), None, None, None),
        check_vma=False,
    )
```

```python
import functools
import math

import jax
import jax.numpy as jnp
import ml_dtypes
import numpy as np
from jax import lax
from jax.experimental import pallas as pl
from jax.experimental.pallas import tpu as pltpu
from jax.sharding import Mesh
from jax.sharding import PartitionSpec as P

FCH = 512
TAPS = 8
AVG = 32
SPEC = 16
SCALE = 1.0 / (AVG * SPEC)


ANY = pl.BlockSpec(memory_space=pl.ANY)
VMEM = pl.BlockSpec(memory_space=pltpu.VMEM)
SMEM = pl.BlockSpec(memory_space=pltpu.SMEM)


def room(mebibytes):
    return pltpu.CompilerParams(vmem_limit_bytes=mebibytes << 20)


def ring_pairs(count, by):
    return [(i, (i + by) % count) for i in range(count)]


def xor_pairs(count, by):
    return [(i, i ^ by) for i in range(count)]


def pfb_window():
    position = np.arange(TAPS * FCH) + 0.5
    taper = np.sin(np.pi * position / (TAPS * FCH)) ** 2
    table = np.sinc(position / FCH - TAPS / 2) * taper
    return table.reshape(TAPS, FCH).astype(np.float32)


def dft_table():
    position = np.arange(FCH)
    angle = (position[:, None] * position[None, :] % FCH) * (2.0 * math.pi / FCH)
    table = np.concatenate([np.cos(angle), -np.sin(angle)], axis=1) / math.sqrt(FCH)
    upper = table.astype(ml_dtypes.bfloat16)
    lower = (table - upper.astype(np.float64)).astype(ml_dtypes.bfloat16)
    return np.concatenate([upper, lower], axis=0)


def pick(stacked, slot):
    return lax.dynamic_index_in_dim(stacked, slot, 0, keepdims=False)


def in_vmem(array):
    return pltpu.with_memory_space_constraint(array, pltpu.VMEM)


def after(array, *others):
    return lax.optimization_barrier((array, *others))[0]


def exchange(pieces, axis):
    count = len(pieces)
    return [pieces[0]] + [
        lax.ppermute(pieces[by], axis, xor_pairs(count, by)) for by in range(1, count)
    ]


def spectra_kernel(samples_any, window_ref, table_any, out_ref, samples_ref, table_ref, *more):
    upper, lower, sems = more
    samples_copy = pltpu.make_async_copy(samples_any, samples_ref, sems.at[0])
    table_copy = pltpu.make_async_copy(table_any, table_ref, sems.at[1])
    samples_copy.start()
    table_copy.start()
    samples_copy.wait()
    rows = samples_ref.shape[0]
    frames = [
        samples_ref[:, f * FCH : (f + 1) * FCH].astype(jnp.float32)
        for f in range(SPEC + TAPS - 1)
    ]
    for t in range(SPEC):
        total = window_ref[0:1, :] * frames[t]
        for tap in range(1, TAPS):
            total = total + window_ref[tap : tap + 1, :] * frames[t + tap]
        here = slice(t * rows, (t + 1) * rows)
        rounded = total.astype(jnp.bfloat16)
        upper[here, :] = rounded
        lower[here, :] = (total - rounded.astype(jnp.float32)).astype(jnp.bfloat16)

    def dot(lhs, rhs):
        return jnp.dot(lhs, rhs, preferred_element_type=jnp.float32)

    table_copy.wait()
    out_ref[...] = (
        dot(upper[...], table_ref[0:FCH, :])
        + dot(upper[...], table_ref[FCH : 2 * FCH, :])
        + dot(lower[...], table_ref[0:FCH, :])
    )


def spectra(samples):
    rows = samples.shape[0]
    table = jnp.asarray(dft_table())
    part = pltpu.VMEM((SPEC * rows, FCH), jnp.bfloat16)
    return pl.pallas_call(
        spectra_kernel,
        in_specs=[ANY, VMEM, ANY],
        out_shape=pltpu.VMEM((SPEC * rows, 2 * FCH), jnp.float32),
        scratch_shapes=[
            pltpu.VMEM(samples.shape, samples.dtype),
            pltpu.VMEM(table.shape, table.dtype),
            part,
            part,
            pltpu.SemaphoreType.DMA((2,)),
        ],
        compiler_params=room(20),
        name="spectra",
    )(
        pltpu.with_memory_space_constraint(samples, pltpu.HBM),
        jnp.asarray(pfb_window()),
        pltpu.with_memory_space_constraint(table, pltpu.HBM),
    )


def quarters(parts, lane):
    joined = parts[3]
    for i in (2, 1, 0):
        joined = jnp.where(lane < (i + 1) * AVG, parts[i], joined)
    return joined


def voltages_kernel(place_ref, spectra_ref, *refs):
    gain_refs, out_ref, gains = refs[0:4], refs[4], refs[5]
    rows = gain_refs[0].shape[1]
    member = place_ref[0]
    lanes = 4 * AVG
    lane = lax.broadcasted_iota(jnp.int32, (rows, lanes), 1)
    for by in range(4):
        gains[member ^ by] = gain_refs[by][...]
    for s in range(4):
        gain = [
            quarters(
                [pltpu.roll(gains[m, part], (m - s) * AVG % lanes, 1) for m in range(4)], lane
            )
            for part in range(2)
        ]
        band = slice(s * lanes, (s + 1) * lanes)
        for first in range(0, SPEC, 4):
            turned_re, turned_im = [], []
            for q in range(4):
                here = slice((first + q) * rows, (first + q + 1) * rows)
                real = spectra_ref[here, band]
                imag = spectra_ref[here, FCH + s * lanes : FCH + (s + 1) * lanes]
                volt_re = gain[0] * real - gain[1] * imag
                volt_im = gain[0] * imag + gain[1] * real
                turned_re.append(pltpu.roll(volt_re, q * AVG, 1) if q else volt_re)
                turned_im.append(pltpu.roll(volt_im, q * AVG, 1) if q else volt_im)
            for m in range(4):
                for part, turned_part in enumerate((turned_re, turned_im)):
                    values = quarters([turned_part[(i - m) % 4] for i in range(4)], lane)
                    start = (part * SPEC + first) * AVG
                    out_ref[s, m, :, start : start + lanes] = values.astype(jnp.bfloat16)


def voltages(member, spectra_here, gain_parts):
    rows = gain_parts[0].shape[1]
    vmem = pl.BlockSpec(memory_space=pltpu.VMEM)
    return pl.pallas_call(
        voltages_kernel,
        in_specs=[pl.BlockSpec(memory_space=pltpu.SMEM)] + [vmem] * 5,
        out_specs=vmem,
        out_shape=pltpu.VMEM((4, 4, rows, 2 * SPEC * AVG), jnp.bfloat16),
        scratch_shapes=[pltpu.VMEM((4,) + gain_parts[0].shape, jnp.float32)],
        compiler_params=room(12),
        name="voltages",
    )(member.reshape(1), in_vmem(spectra_here), *[in_vmem(part) for part in gain_parts])


def turned(block):
    half = block.shape[1] // 2
    return jnp.concatenate([block[:, half:], -block[:, :half]], axis=1)


def local(samples, input_gains):
    team = ("xh", "c")
    member = lax.axis_index(team)
    y_place = lax.axis_index("y")
    z_place = lax.axis_index("z")
    x_place = lax.axis_index("xl")
    members = lax.axis_size(team)
    bins = input_gains.shape[2]
    z_size = lax.axis_size("z")
    rows = samples.shape[0]

    gain_parts = input_gains.reshape(2, members, rows, bins * AVG).transpose(1, 0, 2, 3)
    gain_parts = exchange([pick(gain_parts, member ^ by) for by in range(members)], team)
    formed = voltages(member, spectra(samples), gain_parts)
    formed = formed.reshape(bins * members, rows, -1)
    block = lax.all_to_all(formed, ("y", "xh", "c"), 0, 0, tiled=True)
    block = block.reshape(bins * members * rows, -1)
    height = block.shape[0]
    half = height // 2
    far = 1 - x_place

    def across(piece):
        return lax.ppermute(piece, "xl", ring_pairs(2, 1))

    def onward(piece, by):
        return lax.ppermute(piece, "z", ring_pairs(z_size, by))

    def product(lhs, columns):
        return (
            jnp.einsum("rk,pk->rp", lhs, columns, preferred_element_type=jnp.float32) * SCALE
        )

    def put(values, x, by):
        nonlocal visibility
        values = values.astype(jnp.float32).reshape(2, height, -1)
        nought = jnp.zeros((), jnp.int32)
        start = (x * z_size + (z_place + by) % z_size) * height
        visibility = lax.dynamic_update_slice(visibility, values, (nought, nought, start))

    ahead, behind = {1: onward(block, 1)}, {1: onward(block, -1)}
    other = across(block)
    for step in range(2, z_size // 2):
        ahead[step] = onward(ahead[step - 1], 1)
        behind[step] = onward(behind[step - 1], -1)
    opposite = jnp.concatenate(
        [onward(ahead[step][:half], 1), onward(behind[step][half:], -1)], axis=0
    )

    own_left = jnp.concatenate([block, turned(block)], axis=0)
    other_left = jnp.concatenate([other, turned(other)], axis=0)

    def swap(columns, *waits):
        made = product(other_left, columns).astype(jnp.bfloat16)
        return across(after(made, *waits))

    blocks = []

    def own(columns, by, *waits, x=x_place):
        blocks.append((product(own_left, after(columns, *waits)), x, by))

    own(block, 0)
    given_a1, given_b1 = swap(ahead[1]), swap(behind[1])
    own(other, 0, x=far)
    own(ahead[1], -1)
    given_a2, given_b2 = swap(ahead[2], given_a1), swap(behind[2], given_b1)
    own(behind[1], 1)
    own(ahead[2], -2)
    own(behind[2], 2)
    given_a3, given_b3 = swap(ahead[3], given_a2), swap(behind[3], given_b2)
    own(ahead[3], -3)
    own(behind[3], 3)
    given_4 = swap(opposite, given_a3)
    own(opposite, 4)
    visibility = jnp.zeros((2, height, height * z_size * 2), jnp.float32)
    blocks[0] = (after(blocks[0][0], given_a3), *blocks[0][1:])
    for values, x, by in blocks:
        put(values, x, by)
    put(given_a1, far, -1)
    put(given_b1, far, 1)
    put(given_a2, far, -2)
    put(given_b2, far, 2)
    put(given_a3, far, -3)
    put(given_b3, far, 3)
    put(given_4, far, 4)
    return visibility[None, None]


def solution(mesh):
    fine = Mesh(
        mesh.devices.reshape(2, 8, 4, 2, 2), ("xl", "z", "y", "xh", "c")
    )
    everything = ("xl", "z", "y", "xh", "c")
    return jax.shard_map(
        local,
        mesh=fine,
        in_specs=(P(everything, None), P(None, ("xl", "z", "y"), None, ("xh", "c"))),
        out_specs=P(("xl", "z", "y"), ("xh", "c"), None, None, None),
        check_vma=False,
    )
```

```python
import functools
import math

import jax
import jax.numpy as jnp
import ml_dtypes
import numpy as np
from jax import lax
from jax.experimental import pallas as pl
from jax.experimental.pallas import tpu as pltpu
from jax.sharding import Mesh
from jax.sharding import PartitionSpec as P

FCH = 512
TAPS = 8
AVG = 32
SPEC = 16
SCALE = 1.0 / (AVG * SPEC)


ANY = pl.BlockSpec(memory_space=pl.ANY)
VMEM = pl.BlockSpec(memory_space=pltpu.VMEM)
SMEM = pl.BlockSpec(memory_space=pltpu.SMEM)


def room(mebibytes):
    return pltpu.CompilerParams(vmem_limit_bytes=mebibytes << 20)


def ring_pairs(count, by):
    return [(i, (i + by) % count) for i in range(count)]


def xor_pairs(count, by):
    return [(i, i ^ by) for i in range(count)]


def pfb_window():
    position = np.arange(TAPS * FCH) + 0.5
    taper = np.sin(np.pi * position / (TAPS * FCH)) ** 2
    table = np.sinc(position / FCH - TAPS / 2) * taper
    return table.reshape(TAPS, FCH).astype(np.float32)


def dft_table():
    position = np.arange(FCH)
    angle = (position[:, None] * position[None, :] % FCH) * (2.0 * math.pi / FCH)
    table = np.concatenate([np.cos(angle), -np.sin(angle)], axis=1) / math.sqrt(FCH)
    upper = table.astype(ml_dtypes.bfloat16)
    lower = (table - upper.astype(np.float64)).astype(ml_dtypes.bfloat16)
    return np.concatenate([upper, lower], axis=0)


def pick(stacked, slot):
    return lax.dynamic_index_in_dim(stacked, slot, 0, keepdims=False)


def in_vmem(array):
    return pltpu.with_memory_space_constraint(array, pltpu.VMEM)


def after(array, *others):
    return lax.optimization_barrier((array, *others))[0]


def exchange(pieces, axis):
    count = len(pieces)
    return [pieces[0]] + [
        lax.ppermute(pieces[by], axis, xor_pairs(count, by)) for by in range(1, count)
    ]


def spectra_kernel(samples_any, window_any, table_any, out_ref, samples_ref, *more):
    window_ref, table_ref, upper, lower, sems = more
    samples_copy = pltpu.make_async_copy(samples_any, samples_ref, sems.at[0])
    table_copy = pltpu.make_async_copy(table_any, table_ref, sems.at[1])
    window_copy = pltpu.make_async_copy(window_any, window_ref, sems.at[2])
    samples_copy.start()
    window_copy.start()
    table_copy.start()
    samples_copy.wait()
    window_copy.wait()
    rows = samples_ref.shape[0]
    frames = [
        samples_ref[:, f * FCH : (f + 1) * FCH].astype(jnp.float32)
        for f in range(SPEC + TAPS - 1)
    ]
    for t in range(SPEC):
        total = window_ref[0:1, :] * frames[t]
        for tap in range(1, TAPS):
            total = total + window_ref[tap : tap + 1, :] * frames[t + tap]
        here = slice(t * rows, (t + 1) * rows)
        rounded = total.astype(jnp.bfloat16)
        upper[here, :] = rounded
        lower[here, :] = (total - rounded.astype(jnp.float32)).astype(jnp.bfloat16)

    def dot(lhs, rhs):
        return jnp.dot(lhs, rhs, preferred_element_type=jnp.float32)

    table_copy.wait()
    out_ref[...] = (
        dot(upper[...], table_ref[0:FCH, :])
        + dot(upper[...], table_ref[FCH : 2 * FCH, :])
        + dot(lower[...], table_ref[0:FCH, :])
    )


def spectra(samples):
    rows = samples.shape[0]
    table = jnp.asarray(dft_table())
    part = pltpu.VMEM((SPEC * rows, FCH), jnp.bfloat16)
    return pl.pallas_call(
        spectra_kernel,
        in_specs=[ANY, ANY, ANY],
        out_shape=pltpu.VMEM((SPEC * rows, 2 * FCH), jnp.float32),
        scratch_shapes=[
            pltpu.VMEM(samples.shape, samples.dtype),
            pltpu.VMEM((TAPS, FCH), jnp.float32),
            pltpu.VMEM(table.shape, table.dtype),
            part,
            part,
            pltpu.SemaphoreType.DMA((3,)),
        ],
        compiler_params=room(20),
        name="spectra",
    )(
        pltpu.with_memory_space_constraint(samples, pltpu.HBM),
        pltpu.with_memory_space_constraint(jnp.asarray(pfb_window()), pltpu.HBM),
        pltpu.with_memory_space_constraint(table, pltpu.HBM),
    )


def quarters(parts, lane):
    joined = parts[3]
    for i in (2, 1, 0):
        joined = jnp.where(lane < (i + 1) * AVG, parts[i], joined)
    return joined


def voltages_kernel(place_ref, spectra_ref, *refs):
    gain_refs, out_ref, gains = refs[0:4], refs[4], refs[5]
    rows = gain_refs[0].shape[1]
    member = place_ref[0]
    lanes = 4 * AVG
    lane = lax.broadcasted_iota(jnp.int32, (rows, lanes), 1)
    for by in range(4):
        gains[member ^ by] = gain_refs[by][...]
    for s in range(4):
        gain = [
            quarters(
                [pltpu.roll(gains[m, part], (m - s) * AVG % lanes, 1) for m in range(4)], lane
            )
            for part in range(2)
        ]
        band = slice(s * lanes, (s + 1) * lanes)
        for first in range(0, SPEC, 4):
            turned_re, turned_im = [], []
            for q in range(4):
                here = slice((first + q) * rows, (first + q + 1) * rows)
                real = spectra_ref[here, band]
                imag = spectra_ref[here, FCH + s * lanes : FCH + (s + 1) * lanes]
                volt_re = gain[0] * real - gain[1] * imag
                volt_im = gain[0] * imag + gain[1] * real
                turned_re.append(pltpu.roll(volt_re, q * AVG, 1) if q else volt_re)
                turned_im.append(pltpu.roll(volt_im, q * AVG, 1) if q else volt_im)
            for m in range(4):
                for part, turned_part in enumerate((turned_re, turned_im)):
                    values = quarters([turned_part[(i - m) % 4] for i in range(4)], lane)
                    start = (part * SPEC + first) * AVG
                    out_ref[s, m, :, start : start + lanes] = values.astype(jnp.bfloat16)


def voltages(member, spectra_here, gain_parts):
    rows = gain_parts[0].shape[1]
    vmem = pl.BlockSpec(memory_space=pltpu.VMEM)
    return pl.pallas_call(
        voltages_kernel,
        in_specs=[pl.BlockSpec(memory_space=pltpu.SMEM)] + [vmem] * 5,
        out_specs=vmem,
        out_shape=pltpu.VMEM((4, 4, rows, 2 * SPEC * AVG), jnp.bfloat16),
        scratch_shapes=[pltpu.VMEM((4,) + gain_parts[0].shape, jnp.float32)],
        compiler_params=room(12),
        name="voltages",
    )(member.reshape(1), in_vmem(spectra_here), *[in_vmem(part) for part in gain_parts])


def turned(block):
    half = block.shape[1] // 2
    return jnp.concatenate([block[:, half:], -block[:, :half]], axis=1)


def local(samples, input_gains):
    team = ("xh", "c")
    member = lax.axis_index(team)
    y_place = lax.axis_index("y")
    z_place = lax.axis_index("z")
    x_place = lax.axis_index("xl")
    members = lax.axis_size(team)
    bins = input_gains.shape[2]
    z_size = lax.axis_size("z")
    rows = samples.shape[0]

    gain_parts = input_gains.reshape(2, members, rows, bins * AVG).transpose(1, 0, 2, 3)
    gain_parts = exchange([pick(gain_parts, member ^ by) for by in range(members)], team)
    formed = voltages(member, spectra(samples), gain_parts)
    formed = formed.reshape(bins * members, rows, -1)
    block = lax.all_to_all(formed, ("y", "xh", "c"), 0, 0, tiled=True)
    block = block.reshape(bins * members * rows, -1)
    height = block.shape[0]
    half = height // 2
    far = 1 - x_place

    def across(piece):
        return lax.ppermute(piece, "xl", ring_pairs(2, 1))

    def onward(piece, by):
        return lax.ppermute(piece, "z", ring_pairs(z_size, by))

    def product(lhs, columns):
        return (
            jnp.einsum("rk,pk->rp", lhs, columns, preferred_element_type=jnp.float32) * SCALE
        )

    def put(values, x, by):
        nonlocal visibility
        values = values.astype(jnp.float32).reshape(2, height, -1)
        nought = jnp.zeros((), jnp.int32)
        start = (x * z_size + (z_place + by) % z_size) * height
        visibility = lax.dynamic_update_slice(visibility, values, (nought, nought, start))

    ahead, behind = {1: onward(block, 1)}, {1: onward(block, -1)}
    other = across(block)
    own_left = jnp.concatenate([block, turned(block)], axis=0)
    other_left = jnp.concatenate([other, turned(other)], axis=0)

    def swap(columns, *waits):
        made = product(other_left, columns).astype(jnp.bfloat16)
        return across(after(made, *waits))

    blocks = []

    def own(columns, by, *waits, x=x_place):
        blocks.append((product(own_left, after(columns, *waits)), x, by))

    def move(step, *waits):
        ahead[step] = onward(after(ahead[step - 1], *waits), 1)
        behind[step] = onward(after(behind[step - 1], *waits), -1)

    own(block, 0)
    given_a1, given_b1 = swap(ahead[1]), swap(behind[1])
    move(2)
    own(other, 0, x=far)
    own(ahead[1], -1)
    given_a2, given_b2 = swap(ahead[2], given_a1), swap(behind[2], given_b1)
    own(behind[1], 1)
    own(ahead[2], -2)
    move(3)
    own(behind[2], 2)
    given_a3, given_b3 = swap(ahead[3], given_a2), swap(behind[3], given_b2)
    own(ahead[3], -3, given_a3)
    own(behind[3], 3, given_a3)
    opposite = [
        onward(ahead[3][:half], 1),
        onward(behind[3][half:], -1),
    ]
    opposite = jnp.concatenate(opposite, axis=0)
    given_4 = swap(opposite, given_a3)
    own(opposite, 4)
    visibility = jnp.zeros((2, height, height * z_size * 2), jnp.float32)
    blocks[0] = (after(blocks[0][0], given_a3), *blocks[0][1:])
    for values, x, by in blocks:
        put(values, x, by)
    put(given_a1, far, -1)
    put(given_b1, far, 1)
    put(given_a2, far, -2)
    put(given_b2, far, 2)
    put(given_a3, far, -3)
    put(given_b3, far, 3)
    put(given_4, far, 4)
    return visibility[None, None]


def solution(mesh):
    fine = Mesh(
        mesh.devices.reshape(2, 8, 4, 2, 2), ("xl", "z", "y", "xh", "c")
    )
    everything = ("xl", "z", "y", "xh", "c")
    return jax.shard_map(
        local,
        mesh=fine,
        in_specs=(P(everything, None), P(None, ("xl", "z", "y"), None, ("xh", "c"))),
        out_specs=P(("xl", "z", "y"), ("xh", "c"), None, None, None),
        check_vma=False,
    )
```

```python
import functools
import math

import jax
import jax.numpy as jnp
import ml_dtypes
import numpy as np
from jax import lax
from jax.experimental import pallas as pl
from jax.experimental.pallas import tpu as pltpu
from jax.sharding import Mesh
from jax.sharding import PartitionSpec as P

FCH = 512
TAPS = 8
AVG = 32
SPEC = 16
SCALE = 1.0 / (AVG * SPEC)


ANY = pl.BlockSpec(memory_space=pl.ANY)
VMEM = pl.BlockSpec(memory_space=pltpu.VMEM)
SMEM = pl.BlockSpec(memory_space=pltpu.SMEM)


def room(mebibytes):
    return pltpu.CompilerParams(vmem_limit_bytes=mebibytes << 20)


def ring_pairs(count, by):
    return [(i, (i + by) % count) for i in range(count)]


def xor_pairs(count, by):
    return [(i, i ^ by) for i in range(count)]


def pfb_window():
    position = np.arange(TAPS * FCH) + 0.5
    taper = np.sin(np.pi * position / (TAPS * FCH)) ** 2
    table = np.sinc(position / FCH - TAPS / 2) * taper
    return table.reshape(TAPS, FCH).astype(np.float32)


def dft_table():
    position = np.arange(FCH)
    angle = (position[:, None] * position[None, :] % FCH) * (2.0 * math.pi / FCH)
    table = np.concatenate([np.cos(angle), -np.sin(angle)], axis=1) / math.sqrt(FCH)
    upper = table.astype(ml_dtypes.bfloat16)
    lower = (table - upper.astype(np.float64)).astype(ml_dtypes.bfloat16)
    return np.concatenate([upper, lower], axis=0)


def pick(stacked, slot):
    return lax.dynamic_index_in_dim(stacked, slot, 0, keepdims=False)


def in_vmem(array):
    return pltpu.with_memory_space_constraint(array, pltpu.VMEM)


def after(array, *others):
    return lax.optimization_barrier((array, *others))[0]


def exchange(pieces, axis):
    count = len(pieces)
    return [pieces[0]] + [
        lax.ppermute(pieces[by], axis, xor_pairs(count, by)) for by in range(1, count)
    ]


def spectra_kernel(samples_any, window_any, table_any, out_ref, samples_ref, *more):
    window_ref, table_ref, upper, lower, sems = more
    samples_copy = pltpu.make_async_copy(samples_any, samples_ref, sems.at[0])
    table_copy = pltpu.make_async_copy(table_any, table_ref, sems.at[1])
    window_copy = pltpu.make_async_copy(window_any, window_ref, sems.at[2])
    samples_copy.start()
    window_copy.start()
    table_copy.start()
    samples_copy.wait()
    window_copy.wait()
    rows = samples_ref.shape[0]
    frames = [
        samples_ref[:, f * FCH : (f + 1) * FCH].astype(jnp.float32)
        for f in range(SPEC + TAPS - 1)
    ]
    for t in range(SPEC):
        total = window_ref[0:1, :] * frames[t]
        for tap in range(1, TAPS):
            total = total + window_ref[tap : tap + 1, :] * frames[t + tap]
        here = slice(t * rows, (t + 1) * rows)
        rounded = total.astype(jnp.bfloat16)
        upper[here, :] = rounded
        lower[here, :] = (total - rounded.astype(jnp.float32)).astype(jnp.bfloat16)

    def dot(lhs, rhs):
        return jnp.dot(lhs, rhs, preferred_element_type=jnp.float32)

    table_copy.wait()
    out_ref[...] = (
        dot(upper[...], table_ref[0:FCH, :])
        + dot(upper[...], table_ref[FCH : 2 * FCH, :])
        + dot(lower[...], table_ref[0:FCH, :])
    )


def spectra(samples):
    rows = samples.shape[0]
    table = jnp.asarray(dft_table())
    part = pltpu.VMEM((SPEC * rows, FCH), jnp.bfloat16)
    return pl.pallas_call(
        spectra_kernel,
        in_specs=[ANY, ANY, ANY],
        out_shape=pltpu.VMEM((SPEC * rows, 2 * FCH), jnp.float32),
        scratch_shapes=[
            pltpu.VMEM(samples.shape, samples.dtype),
            pltpu.VMEM((TAPS, FCH), jnp.float32),
            pltpu.VMEM(table.shape, table.dtype),
            part,
            part,
            pltpu.SemaphoreType.DMA((3,)),
        ],
        compiler_params=room(20),
        name="spectra",
    )(
        pltpu.with_memory_space_constraint(samples, pltpu.HBM),
        pltpu.with_memory_space_constraint(jnp.asarray(pfb_window()), pltpu.HBM),
        pltpu.with_memory_space_constraint(table, pltpu.HBM),
    )


def quarters(parts, lane):
    joined = parts[3]
    for i in (2, 1, 0):
        joined = jnp.where(lane < (i + 1) * AVG, parts[i], joined)
    return joined


def voltages_kernel(place_ref, spectra_ref, *refs):
    gain_refs, out_ref, gains = refs[0:4], refs[4], refs[5]
    rows = gain_refs[0].shape[1]
    member = place_ref[0]
    lanes = 4 * AVG
    lane = lax.broadcasted_iota(jnp.int32, (rows, lanes), 1)
    for by in range(4):
        gains[member ^ by] = gain_refs[by][...]
    for s in range(4):
        gain = [
            quarters(
                [pltpu.roll(gains[m, part], (m - s) * AVG % lanes, 1) for m in range(4)], lane
            )
            for part in range(2)
        ]
        band = slice(s * lanes, (s + 1) * lanes)
        for first in range(0, SPEC, 4):
            turned_re, turned_im = [], []
            for q in range(4):
                here = slice((first + q) * rows, (first + q + 1) * rows)
                real = spectra_ref[here, band]
                imag = spectra_ref[here, FCH + s * lanes : FCH + (s + 1) * lanes]
                volt_re = gain[0] * real - gain[1] * imag
                volt_im = gain[0] * imag + gain[1] * real
                turned_re.append(pltpu.roll(volt_re, q * AVG, 1) if q else volt_re)
                turned_im.append(pltpu.roll(volt_im, q * AVG, 1) if q else volt_im)
            for m in range(4):
                for part, turned_part in enumerate((turned_re, turned_im)):
                    values = quarters([turned_part[(i - m) % 4] for i in range(4)], lane)
                    start = (part * SPEC + first) * AVG
                    out_ref[s, m, :, start : start + lanes] = values.astype(jnp.bfloat16)


def voltages(member, spectra_here, gain_parts):
    rows = gain_parts[0].shape[1]
    vmem = pl.BlockSpec(memory_space=pltpu.VMEM)
    return pl.pallas_call(
        voltages_kernel,
        in_specs=[pl.BlockSpec(memory_space=pltpu.SMEM)] + [vmem] * 5,
        out_specs=vmem,
        out_shape=pltpu.VMEM((4, 4, rows, 2 * SPEC * AVG), jnp.bfloat16),
        scratch_shapes=[pltpu.VMEM((4,) + gain_parts[0].shape, jnp.float32)],
        compiler_params=room(12),
        name="voltages",
    )(member.reshape(1), in_vmem(spectra_here), *[in_vmem(part) for part in gain_parts])


def turned(block):
    half = block.shape[1] // 2
    return jnp.concatenate([block[:, half:], -block[:, :half]], axis=1)


def local(samples, input_gains):
    team = ("xh", "c")
    member = lax.axis_index(team)
    y_place = lax.axis_index("y")
    z_place = lax.axis_index("z")
    x_place = lax.axis_index("xl")
    members = lax.axis_size(team)
    bins = input_gains.shape[2]
    z_size = lax.axis_size("z")
    rows = samples.shape[0]

    gain_parts = input_gains.reshape(2, members, rows, bins * AVG).transpose(1, 0, 2, 3)
    gain_parts = exchange([pick(gain_parts, member ^ by) for by in range(members)], team)
    formed = voltages(member, spectra(samples), gain_parts)
    formed = formed.reshape(bins * members, rows, -1)
    block = lax.all_to_all(formed, ("y", "xh", "c"), 0, 0, tiled=True)
    block = block.reshape(bins * members * rows, -1)
    height = block.shape[0]
    half = height // 2
    far = 1 - x_place

    def across(piece):
        return lax.ppermute(piece, "xl", ring_pairs(2, 1))

    def onward(piece, by):
        return lax.ppermute(piece, "z", ring_pairs(z_size, by))

    def product(lhs, columns):
        return (
            jnp.einsum("rk,pk->rp", lhs, columns, preferred_element_type=jnp.float32) * SCALE
        )

    def put(values, x, by):
        nonlocal visibility
        values = values.astype(jnp.float32).reshape(2, height, -1)
        nought = jnp.zeros((), jnp.int32)
        start = (x * z_size + (z_place + by) % z_size) * height
        visibility = lax.dynamic_update_slice(visibility, values, (nought, nought, start))

    ahead, behind = {1: onward(block, 1)}, {1: onward(block, -1)}
    other = across(block)
    own_left = jnp.concatenate([block, turned(block)], axis=0)
    other_left = jnp.concatenate([other, turned(other)], axis=0)

    def swap(columns, *waits):
        made = product(other_left, columns).astype(jnp.bfloat16)
        return across(after(made, *waits))

    blocks = []

    def own(columns, by, *waits, x=x_place):
        blocks.append((product(own_left, after(columns, *waits)), x, by))

    def move(step, *waits):
        ahead[step] = onward(after(ahead[step - 1], *waits), 1)
        behind[step] = onward(after(behind[step - 1], *waits), -1)

    own(block, 0)
    given_a1, given_b1 = swap(ahead[1]), swap(behind[1])
    move(2)
    own(other, 0, x=far)
    own(ahead[1], -1)
    given_a2, given_b2 = swap(ahead[2], given_a1), swap(behind[2], given_b1)
    own(behind[1], 1)
    own(ahead[2], -2)
    move(3)
    own(behind[2], 2)
    given_a3, given_b3 = swap(after(ahead[3], given_a2)), swap(after(behind[3], given_b2))
    own(ahead[3], -3, given_a3)
    own(behind[3], 3, given_a3)
    opposite = [
        onward(ahead[3][:half], 1),
        onward(behind[3][half:], -1),
    ]
    opposite = jnp.concatenate(opposite, axis=0)
    made = product(other_left, opposite).astype(jnp.bfloat16)
    given_4 = across(after(made, given_a3))
    own(opposite, 4, made)
    visibility = jnp.zeros((2, height, height * z_size * 2), jnp.float32)
    blocks[0] = (after(blocks[0][0], given_a3), *blocks[0][1:])
    for values, x, by in blocks:
        put(values, x, by)
    put(given_a1, far, -1)
    put(given_b1, far, 1)
    put(given_a2, far, -2)
    put(given_b2, far, 2)
    put(given_a3, far, -3)
    put(given_b3, far, 3)
    put(given_4, far, 4)
    return visibility[None, None]


def solution(mesh):
    fine = Mesh(
        mesh.devices.reshape(2, 8, 4, 2, 2), ("xl", "z", "y", "xh", "c")
    )
    everything = ("xl", "z", "y", "xh", "c")
    return jax.shard_map(
        local,
        mesh=fine,
        in_specs=(P(everything, None), P(None, ("xl", "z", "y"), None, ("xh", "c"))),
        out_specs=P(("xl", "z", "y"), ("xh", "c"), None, None, None),
        check_vma=False,
    )
```
